512 devices in a mesh: ctx: 32 (over x, y), tp: 16 (over z, core).
Axes of the slice: x: 4, y: 8, z: 8, core: 2. Of those that a mesh axis runs over, the one named last changes fastest.
Arguments:
- tokens: bfloat16 [4096, 4096], P('ctx', 'tp'), may hold values from -6 to 6
- gate_values: bfloat16 [4096, 4096], P('ctx', 'tp'), may hold values from -6 to 6
- filters: bfloat16 [4096, 4096], P('ctx', 'tp'), may hold values from -1 to 1
- input_weight: bfloat16 [4096, 4096], P('ctx', 'tp'), may hold values from -0.09375 to 0.09375
- output_weight: bfloat16 [4096, 4096], P('tp', 'ctx'), may hold values from -0.09375 to 0.09375
- cotangent: bfloat16 [4096, 4096], P('ctx', 'tp'), may hold values from -6 to 6
Outputs:
- layer_output: bfloat16 [4096, 4096], P('ctx', 'tp')
- grad_tokens: bfloat16 [4096, 4096], P('ctx', 'tp')
- grad_gate: bfloat16 [4096, 4096], P('ctx', 'tp')
- grad_input_weight: bfloat16 [4096, 4096], P('ctx', 'tp')
- grad_output_weight: bfloat16 [4096, 4096], P('tp', 'ctx')
The draws below stay inside these ranges and needn't reach their ends.
All inputs are finite; a program needn't handle non-finite values.
Results may differ from the reference program's by a relative error of at most 0.028.
Values may be sent and summed in bfloat16 or wider, within the bound.
No kernel may reach another device: no remote copies, remote signals or barrier semaphores. Data moves between devices by JAX's collectives and lax.ppermute only.
A program may use at most 64 MiB of HBM per device.

```python
import math
import jax
import jax.numpy as jnp
from jax import lax

D = 4096
C = 4096
SEQ = 4096
N_CTX = 32
N_TP = 16


def draw_filters(key, part):
    key = jax.random.fold_in(key, 11)
    rate_key, noise_key = jax.random.split(key)
    rates = jnp.exp(jax.random.uniform(rate_key, (C,), jnp.float32, math.log(0.3), math.log(40.0)))
    noise = jnp.clip(jax.random.normal(noise_key, (SEQ, C), jnp.float32), -4.0, 4.0)
    position = jnp.arange(SEQ, dtype=jnp.float32)[:, None] / SEQ
    decay = jnp.exp(-rates[None, :] * position)
    return (noise * decay * (3.0 / math.sqrt(SEQ))).astype(jnp.bfloat16)


def raised(entries, stream_key, source, target, blocks, factor):
    owner, partner = [(jnp.arange(entries.shape[dim]) // (entries.shape[dim] // blocks)).reshape([-1 if axis == dim else 1 for axis in range(entries.ndim)]) for dim in (source, target)]
    chosen = jax.random.permutation(stream_key, blocks)[partner]
    strong = (owner == chosen) | (owner == (partner + blocks // 2) % blocks)
    return jnp.where(strong, factor * entries, entries)


def shard_levels(own_key, shape, shards, least, top_value):
    level, own = 1.0, jax.random.fold_in(own_key, 6)
    for dim, shards_of in shards:
        heights = jnp.exp(jax.random.uniform(jax.random.fold_in(own, dim), (shards_of,), jnp.float32, least / len(shards), top_value / len(shards)))
        level = level * jnp.repeat(heights, shape[dim] // shards_of).reshape([-1 if axis == dim else 1 for axis in range(len(shape))])
    return level


def gaussian(rng, dims, deviation, limit, cuts=(), kind=jnp.bfloat16):
    values = deviation * jax.random.normal(rng, dims, jnp.float32)
    if cuts:
        values = values * shard_levels(rng, dims, cuts, -0.22, 0.18)
    return jnp.clip(values, -limit, limit).astype(kind)


def heavy_noise(key, extent, deviation, limit, cuts, heavy, held_as=jnp.bfloat16):
    drawn = deviation * jax.random.normal(key, extent, jnp.float32)
    if cuts:
        drawn = drawn * shard_levels(key, extent, cuts, -0.22, 0.18)
    return jnp.clip(raised(drawn, jax.random.fold_in(key, 3), *heavy), -limit, limit).astype(held_as)


def setup_inputs(seed: int = 0) -> dict:
    splits = jax.random.split(jax.random.key(seed), 7)
    return {
        "tokens": heavy_noise(splits[0], (SEQ, D), 1.0, 6.0, ((0, 32), (1, 16)), (0, 1, 32, 2.75)),
        "gate_values": gaussian(splits[1], (SEQ, C), 1.0, 6.0, ((0, 32), (1, 16))),
        "filters": draw_filters(jax.random.fold_in(splits[6], 71), 0),
        "input_weight": gaussian(splits[3], (D, C), D ** -0.5, 0.09375, ((0, 32), (1, 16))),
        "output_weight": gaussian(splits[4], (C, D), C ** -0.5, 0.09375, ((0, 16), (1, 32))),
        "cotangent": gaussian(splits[5], (SEQ, D), 1.0, 6.0, ((0, 32), (1, 16))),
    }


def as_float(array):
    return array.astype(jnp.float32)


def convolve(values, kernel, adjoint):
    length = values.shape[0]
    spectrum = jnp.fft.rfft(values, n=2 * length, axis=0)
    response = jnp.fft.rfft(kernel, n=2 * length, axis=0)
    if adjoint:
        response = jnp.conj(response)
    result = jnp.fft.irfft(spectrum * response, n=2 * length, axis=0)
    return result[:length].astype(jnp.float32)


def blocked_product(left, right, groups):
    width = left.shape[1] // groups
    result = jnp.zeros((left.shape[0], right.shape[1]), jnp.float32)
    for group in range(groups):
        partial_sum = jnp.dot(as_float(left[:, group * width:(group + 1) * width]),
                              as_float(right[group * width:(group + 1) * width]),
                              preferred_element_type=jnp.float32)
        rounded = lax.optimization_barrier(partial_sum.astype(jnp.bfloat16))
        result = result + as_float(rounded)
    return result


def reference(tokens, gate_values, filters, input_weight, output_weight, cotangent):
    kernel = as_float(filters)
    projected = jnp.dot(as_float(tokens), as_float(input_weight), preferred_element_type=jnp.float32).astype(jnp.bfloat16)
    convolved = convolve(as_float(projected), kernel, False)
    modulated = (as_float(gate_values) * convolved).astype(jnp.bfloat16)
    layer_output = blocked_product(modulated, output_weight, N_TP).astype(jnp.bfloat16)
    grad_modulated = jnp.dot(as_float(cotangent), as_float(output_weight).T, preferred_element_type=jnp.float32)
    grad_gate = (grad_modulated * convolved).astype(jnp.bfloat16)
    grad_convolved = (grad_modulated * as_float(gate_values)).astype(jnp.bfloat16)
    grad_projected = convolve(as_float(grad_convolved), kernel, True).astype(jnp.bfloat16)
    grad_tokens = blocked_product(grad_projected, input_weight.T, N_TP).astype(jnp.bfloat16)
    grad_input_weight = blocked_product(tokens.T, grad_projected, N_CTX).astype(jnp.bfloat16)
    grad_output_weight = jnp.dot(as_float(modulated).T, as_float(cotangent), preferred_element_type=jnp.float32).astype(jnp.bfloat16)
    return layer_output, grad_tokens, grad_gate, grad_input_weight, grad_output_weight
```

```python
import math

import jax
import jax.numpy as jnp
import numpy as np
from jax import lax
from jax.experimental import pallas as pl
from jax.experimental.pallas import tpu as pltpu
from jax.sharding import Mesh, PartitionSpec as P

bf16 = jnp.bfloat16
f32 = jnp.float32

NX, NY, NH, NL, NC = 4, 8, 4, 2, 2
CTX = ("x", "y")
TP = ("zh", "zl", "core")
ALL = CTX + TP
Z = ("zh", "zl")

BLOCKS = NX * NY
ROWS = 128
FREQS = 2 * BLOCKS
LENGTH = FREQS * ROWS
OWN = 8

VMEM = pl.BlockSpec(memory_space=pltpu.VMEM)
SMEM = pl.BlockSpec(memory_space=pltpu.SMEM)
PARAMS = pltpu.CompilerParams(vmem_limit_bytes=48 * 1024 * 1024)


def swap_pairs():
    def place(x, y, h, l, c):
        return (((x * NY + y) * NH + h) * NL + l) * NC + c

    return [
        (place(x, y, h, l, c), place(h, y, x, l, c))
        for x in range(NX)
        for y in range(NY)
        for h in range(NH)
        for l in range(NL)
        for c in range(NC)
    ]


def tables():
    freq = np.arange(FREQS)
    block = np.arange(BLOCKS)
    row = np.arange(ROWS)
    angle = 2 * math.pi * (freq[:, None] * block[None, :] % FREQS) / FREQS
    first = np.concatenate([np.cos(angle), -np.sin(angle)], 0)
    twist = 2 * math.pi * (freq[:, None] * row[None, :] % LENGTH) / LENGTH
    angle = 2 * math.pi * (row[:, None] * row[None, :] % ROWS) / ROWS
    cosine, sine = np.cos(angle), np.sin(angle)
    second = np.block([[cosine, -sine], [sine, cosine]])
    return (
        jnp.asarray(first, bf16),
        jnp.asarray(first.T, bf16),
        jnp.asarray(np.cos(twist), f32),
        jnp.asarray(np.sin(twist), f32),
        jnp.asarray(second, bf16),
        jnp.asarray(second.T, bf16),
    )


def dot(left, right):
    return jnp.dot(left, right, preferred_element_type=f32)


def weight_block(weights, which, l, c):
    first = 4 * l + 2 * c
    return jnp.concatenate([weights[first, which], weights[first + 1, which]], 0)


def project_kernel(me_ref, own, other, weights, filters, gate, out):
    me = me_ref[0]
    for which in range(2):
        total = None
        for l in range(NL):
            for held, c in ((own, me), (other, 1 - me)):
                rows = held[:, l, which].reshape(NX * ROWS, 2 * ROWS)
                term = dot(rows, weight_block(weights, which, l, c))
                total = term if total is None else total + term
        out[:, which * NX * ROWS : (which + 1) * NX * ROWS] = total.T.astype(bf16)
    base = 2 * NX * ROWS
    out[:, base : base + ROWS] = filters[...].astype(f32).T.astype(bf16)
    out[:, base + ROWS : base + 2 * ROWS] = gate[...].astype(f32).T.astype(bf16)


def convolve_kernel(
    got, first, first_back, twist_cos, twist_sin, second, second_back, out,
    proj, gmod, filt, gate, mixed, spectrum, product, back, o_mod, o_gp, o_gg,
):
    half = NX * ROWS

    def lanes(start):
        return slice(start, start + ROWS)

    for y in range(NY):
        for x in range(NX):
            b = x * NY + y
            at = slice(b * OWN, (b + 1) * OWN)
            for base, held in ((0, proj), (half, gmod)):
                total = got[y, :, lanes(base + x * ROWS)].astype(f32)
                for k in range(1, NX):
                    total = total + got[k * NY + y, :, lanes(base + x * ROWS)].astype(f32)
                held[at, :] = total
            filt[at, :] = got[b, :, lanes(2 * half)].astype(f32)
            gate[at, :] = got[b, :, lanes(2 * half + ROWS)].astype(f32)
    cosine, sine = twist_cos[...], twist_sin[...]
    for c in range(OWN):
        pick = pl.ds(c, BLOCKS, stride=OWN)
        signals = jnp.concatenate(
            [
                proj[pick, :].astype(bf16),
                (gmod[pick, :] * gate[pick, :]).astype(bf16),
                filt[pick, :].astype(bf16),
            ],
            1,
        )
        parts = dot(first[...], signals)
        for i in range(3):
            real = parts[:FREQS, lanes(i * ROWS)]
            imag = parts[FREQS:, lanes(i * ROWS)]
            at = slice((c * 3 + i) * FREQS, (c * 3 + i + 1) * FREQS)
            mixed[at, :ROWS] = (real * cosine + imag * sine).astype(bf16)
            mixed[at, ROWS:] = (imag * cosine - real * sine).astype(bf16)
    spectrum[...] = dot(mixed[...], second[...])
    for c in range(OWN):
        (xr, xi), (gr, gi), (hr, hi) = [
            (spectrum[at, :ROWS], spectrum[at, ROWS:])
            for at in [slice((c * 3 + i) * FREQS, (c * 3 + i + 1) * FREQS) for i in range(3)]
        ]
        at = slice(2 * c * FREQS, (2 * c + 1) * FREQS)
        product[at, :ROWS] = (xr * hr - xi * hi).astype(bf16)
        product[at, ROWS:] = (xr * hi + xi * hr).astype(bf16)
        at = slice((2 * c + 1) * FREQS, (2 * c + 2) * FREQS)
        product[at, :ROWS] = (gr * hr + gi * hi).astype(bf16)
        product[at, ROWS:] = (gi * hr - gr * hi).astype(bf16)
    back[...] = dot(product[...], second_back[...])
    for c in range(OWN):
        pick = pl.ds(c, BLOCKS, stride=OWN)
        columns = []
        for i in range(2):
            at = slice((2 * c + i) * FREQS, (2 * c + i + 1) * FREQS)
            real, imag = back[at, :ROWS], back[at, ROWS:]
            columns.append(
                jnp.concatenate(
                    [
                        (real * cosine - imag * sine).astype(bf16),
                        (imag * cosine + real * sine).astype(bf16),
                    ],
                    0,
                )
            )
        in_time = dot(first_back[...], jnp.concatenate(columns, 1)) * (1.0 / LENGTH)
        convolved = in_time[:, :ROWS]
        o_gp[pick, :] = in_time[:, ROWS:]
        o_mod[pick, :] = gate[pick, :] * convolved
        o_gg[pick, :] = gmod[pick, :] * convolved
    for y in range(NY):
        for x in range(NX):
            b = x * NY + y
            at = slice(b * OWN, (b + 1) * OWN)
            modulated = o_mod[at, :].astype(bf16)
            grad = o_gp[at, :].astype(bf16)
            for k in range(NX):
                out[k * NY + y, :, lanes(x * ROWS)] = modulated
                out[k * NY + y, :, lanes(half + x * ROWS)] = grad
            out[b, :, lanes(2 * half)] = o_gg[at, :].astype(bf16)


def weight_grad_kernel(me_ref, got, own, other, out):
    me = me_ref[0]
    half = NX * ROWS
    for which in range(2):
        left = got[:, half:] if which == 0 else got[:, :half]
        for l in range(NL):
            for held, c in ((own, me), (other, 1 - me)):
                rows = held[:, l, which].reshape(half, 2 * ROWS)
                total = dot(left, rows).astype(bf16)
                out[4 * l + 2 * c, which] = total[:, :ROWS]
                out[4 * l + 2 * c + 1, which] = total[:, ROWS:]


def output_kernel(me_ref, got, weights, keep, send):
    me = me_ref[0]
    half = NX * ROWS
    for which in range(2):
        start = which * half
        rows = got[:, start : start + half].astype(f32).T.astype(bf16)
        for l in range(NL):
            for held, c in ((keep, me), (send, 1 - me)):
                block = weight_block(weights, 1 - which, l, c)
                total = lax.dot_general(
                    rows, block, (((1,), (1,)), ((), ())), preferred_element_type=f32
                )
                held[:, l, which] = total.astype(bf16).reshape(NX, ROWS, 2 * ROWS)


def call(kernel, inputs, out_shape, flops, scratch=(), first_smem=True):
    specs = [VMEM] * len(inputs)
    if first_smem:
        specs[0] = SMEM
    many = isinstance(out_shape, tuple)
    return pl.pallas_call(
        kernel,
        out_shape=out_shape,
        in_specs=specs,
        out_specs=(VMEM,) * len(out_shape) if many else VMEM,
        scratch_shapes=list(scratch),
        compiler_params=PARAMS,
        cost_estimate=pl.CostEstimate(
            flops=flops,
            bytes_accessed=sum(a.size * a.dtype.itemsize for a in inputs),
            transcendentals=0,
        ),
    )(*inputs)


def on_device(tokens, gate_values, filters, input_weight, output_weight, cotangent):
    tokens_here, features = tokens.shape
    channels = gate_values.shape[1]
    me = lax.axis_index("core").astype(jnp.int32).reshape(1)
    swap = swap_pairs()

    weights = lax.all_gather(jnp.stack([input_weight, output_weight.T]), "y", axis=0)
    moved = jnp.stack([lax.ppermute(tokens, ALL, swap), lax.ppermute(cotangent, ALL, swap)])
    copies = jnp.broadcast_to(moved[None], (NH * NL, 2, tokens_here, features))
    own = lax.all_to_all(copies, Z, split_axis=0, concat_axis=0, tiled=True)
    other = lax.ppermute(own, "core", [(0, 1), (1, 0)])
    held = (NH, NL, 2, tokens_here, features)
    own, other = own.reshape(held), other.reshape(held)

    half = NX * ROWS
    sent = call(
        project_kernel,
        (me, own, other, weights, filters, gate_values),
        jax.ShapeDtypeStruct((channels, 2 * half + 2 * ROWS), bf16),
        4 * half * 1024 * channels,
    )
    got = lax.all_to_all(
        sent.reshape(BLOCKS, OWN, 2 * half + 2 * ROWS), CTX, split_axis=0, concat_axis=0, tiled=True
    )
    per_channel = pltpu.VMEM((BLOCKS * OWN, ROWS), f32)
    sent = call(
        convolve_kernel,
        (got,) + tables(),
        jax.ShapeDtypeStruct((BLOCKS, OWN, 2 * half + ROWS), bf16),
        2 * 40 * OWN * FREQS * 256 * 256,
        [per_channel] * 4
        + [
            pltpu.VMEM((3 * OWN * FREQS, 2 * ROWS), bf16),
            pltpu.VMEM((3 * OWN * FREQS, 2 * ROWS), f32),
            pltpu.VMEM((2 * OWN * FREQS, 2 * ROWS), bf16),
            pltpu.VMEM((2 * OWN * FREQS, 2 * ROWS), f32),
        ]
        + [per_channel] * 3,
        first_smem=False,
    )
    got = lax.all_to_all(sent, CTX, split_axis=0, concat_axis=0, tiled=True)
    got = got.reshape(channels, 2 * half + ROWS)
    streams, grad_gate = got[:, : 2 * half], got[:, 2 * half :].T

    grads = call(
        weight_grad_kernel,
        (me, streams, own, other),
        jax.ShapeDtypeStruct((NY, 2, channels, ROWS), bf16),
        4 * half * 1024 * channels,
    )
    grads = lax.psum_scatter(grads, "y", scatter_dimension=0, tiled=True)
    grad_input_weight, grad_output_weight = grads[0, 0].T, grads[0, 1]

    shape = jax.ShapeDtypeStruct(held, bf16)
    keep, send = call(
        output_kernel, (me, streams, weights), (shape, shape), 4 * half * 1024 * channels
    )
    arrived = lax.ppermute(send, "core", [(0, 1), (1, 0)])
    parts = (keep.astype(f32) + arrived.astype(f32)).astype(bf16)
    parts = lax.all_to_all(
        parts.reshape(NH * NL, 2, tokens_here, features), Z, split_axis=0, concat_axis=0, tiled=True
    )
    total = jnp.sum(parts.astype(f32), 0).astype(bf16)
    layer_output = lax.ppermute(total[0], ALL, swap)
    grad_tokens = lax.ppermute(total[1], ALL, swap)
    return (layer_output, grad_tokens, grad_gate, grad_input_weight, grad_output_weight)


def solution(mesh):
    chips = Mesh(mesh.devices.reshape(NX, NY, NH, NL, NC), ALL)
    rows, columns = P(CTX, TP), P(TP, CTX)
    return jax.shard_map(
        on_device,
        mesh=chips,
        in_specs=(rows, rows, rows, rows, columns, rows),
        out_specs=(rows, rows, rows, rows, columns),
        check_vma=False,
    )
```

```python
import math

import jax
import jax.numpy as jnp
import numpy as np
from jax import lax
from jax.experimental import pallas as pl
from jax.experimental.pallas import tpu as pltpu
from jax.sharding import Mesh, PartitionSpec as P

bf16 = jnp.bfloat16
f32 = jnp.float32

NX, NY, NH, NL, NC = 4, 8, 4, 2, 2
CTX = ("x", "y")
TP = ("zh", "zl", "core")
ALL = CTX + TP
Z = ("zh", "zl")

BLOCKS = NX * NY
ROWS = 128
FREQS = 2 * BLOCKS
LENGTH = FREQS * ROWS
OWN = 8

VMEM = pl.BlockSpec(memory_space=pltpu.VMEM)
SMEM = pl.BlockSpec(memory_space=pltpu.SMEM)
PARAMS = pltpu.CompilerParams(vmem_limit_bytes=48 * 1024 * 1024)


def swap_pairs():
    def place(x, y, h, l, c):
        return (((x * NY + y) * NH + h) * NL + l) * NC + c

    return [
        (place(x, y, h, l, c), place(h, y, x, l, c))
        for x in range(NX)
        for y in range(NY)
        for h in range(NH)
        for l in range(NL)
        for c in range(NC)
    ]


def tables():
    freq = np.arange(FREQS)
    block = np.arange(BLOCKS)
    row = np.arange(ROWS)
    angle = 2 * math.pi * (freq[:, None] * block[None, :] % FREQS) / FREQS
    first = np.concatenate([np.cos(angle), -np.sin(angle)], 0)
    twist = 2 * math.pi * (freq[:, None] * row[None, :] % LENGTH) / LENGTH
    angle = 2 * math.pi * (row[:, None] * row[None, :] % ROWS) / ROWS
    cosine, sine = np.cos(angle), np.sin(angle)
    second = np.block([[cosine, -sine], [sine, cosine]])
    return (
        jnp.asarray(first, bf16),
        jnp.asarray(first.T, bf16),
        jnp.asarray(np.cos(twist), f32),
        jnp.asarray(np.sin(twist), f32),
        jnp.asarray(second, bf16),
        jnp.asarray(second.T, bf16),
    )


def dot(left, right):
    return jnp.dot(left, right, preferred_element_type=f32)


def weight_block(weights, which, l, c):
    first = 4 * l + 2 * c
    return jnp.concatenate([weights[first, which], weights[first + 1, which]], 0)


def project_kernel(me_ref, own, other, weights, filters, gate, out):
    me = me_ref[0]
    for which in range(2):
        total = None
        for l in range(NL):
            for held, c in ((own, me), (other, 1 - me)):
                rows = held[:, l, which].reshape(NX * ROWS, 2 * ROWS)
                term = dot(rows, weight_block(weights, which, l, c))
                total = term if total is None else total + term
        out[:, which * NX * ROWS : (which + 1) * NX * ROWS] = total.T.astype(bf16)
    base = 2 * NX * ROWS
    out[:, base : base + ROWS] = filters[...].astype(f32).T.astype(bf16)
    out[:, base + ROWS : base + 2 * ROWS] = gate[...].astype(f32).T.astype(bf16)


def convolve_kernel(
    got, first, first_back, twist_cos, twist_sin, second, second_back, out,
    proj, gmod, filt, gate, mixed, spectrum, product, back, o_mod, o_gp, o_gg,
):
    half = NX * ROWS

    def lanes(start):
        return slice(start, start + ROWS)

    for y in range(NY):
        for x in range(NX):
            b = x * NY + y
            at = slice(b * OWN, (b + 1) * OWN)
            for base, held in ((0, proj), (half, gmod)):
                total = got[y, :, lanes(base + x * ROWS)].astype(f32)
                for k in range(1, NX):
                    total = total + got[k * NY + y, :, lanes(base + x * ROWS)].astype(f32)
                held[at, :] = total
            filt[at, :] = got[b, :, lanes(2 * half)].astype(f32)
            gate[at, :] = got[b, :, lanes(2 * half + ROWS)].astype(f32)
    cosine, sine = twist_cos[...], twist_sin[...]
    for c in range(OWN):
        pick = pl.ds(c, BLOCKS, stride=OWN)
        signals = jnp.concatenate(
            [
                proj[pick, :].astype(bf16),
                (gmod[pick, :] * gate[pick, :]).astype(bf16),
                filt[pick, :].astype(bf16),
            ],
            1,
        )
        parts = dot(first[...], signals)
        for i in range(3):
            real = parts[:FREQS, lanes(i * ROWS)]
            imag = parts[FREQS:, lanes(i * ROWS)]
            at = slice((c * 3 + i) * FREQS, (c * 3 + i + 1) * FREQS)
            mixed[at, :ROWS] = (real * cosine + imag * sine).astype(bf16)
            mixed[at, ROWS:] = (imag * cosine - real * sine).astype(bf16)
    spectrum[...] = dot(mixed[...], second[...])
    for c in range(OWN):
        (xr, xi), (gr, gi), (hr, hi) = [
            (spectrum[at, :ROWS], spectrum[at, ROWS:])
            for at in [slice((c * 3 + i) * FREQS, (c * 3 + i + 1) * FREQS) for i in range(3)]
        ]
        at = slice(2 * c * FREQS, (2 * c + 1) * FREQS)
        product[at, :ROWS] = (xr * hr - xi * hi).astype(bf16)
        product[at, ROWS:] = (xr * hi + xi * hr).astype(bf16)
        at = slice((2 * c + 1) * FREQS, (2 * c + 2) * FREQS)
        product[at, :ROWS] = (gr * hr + gi * hi).astype(bf16)
        product[at, ROWS:] = (gi * hr - gr * hi).astype(bf16)
    back[...] = dot(product[...], second_back[...])
    for c in range(OWN):
        pick = pl.ds(c, BLOCKS, stride=OWN)
        columns = []
        for i in range(2):
            at = slice((2 * c + i) * FREQS, (2 * c + i + 1) * FREQS)
            real, imag = back[at, :ROWS], back[at, ROWS:]
            columns.append(
                jnp.concatenate(
                    [
                        (real * cosine - imag * sine).astype(bf16),
                        (imag * cosine + real * sine).astype(bf16),
                    ],
                    0,
                )
            )
        in_time = dot(first_back[...], jnp.concatenate(columns, 1)) * (1.0 / LENGTH)
        convolved = in_time[:, :ROWS]
        o_gp[pick, :] = in_time[:, ROWS:]
        o_mod[pick, :] = gate[pick, :] * convolved
        o_gg[pick, :] = gmod[pick, :] * convolved
    for y in range(NY):
        for x in range(NX):
            b = x * NY + y
            at = slice(b * OWN, (b + 1) * OWN)
            modulated = o_mod[at, :].astype(bf16)
            grad = o_gp[at, :].astype(bf16)
            for k in range(NX):
                out[k * NY + y, :, lanes(x * ROWS)] = modulated
                out[k * NY + y, :, lanes(half + x * ROWS)] = grad
            out[b, :, lanes(2 * half)] = o_gg[at, :].astype(bf16)


def weight_grad_kernel(me_ref, got, own, other, out):
    me = me_ref[0]
    half = NX * ROWS
    for which in range(2):
        left = got[:, half:] if which == 0 else got[:, :half]
        for l in range(NL):
            for held, c in ((own, me), (other, 1 - me)):
                rows = held[:, l, which].reshape(half, 2 * ROWS)
                total = dot(left, rows).astype(bf16)
                out[4 * l + 2 * c, which] = total[:, :ROWS]
                out[4 * l + 2 * c + 1, which] = total[:, ROWS:]


def output_kernel(me_ref, got, weights, keep, send):
    me = me_ref[0]
    half = NX * ROWS
    for which in range(2):
        start = which * half
        rows = got[:, start : start + half].astype(f32).T.astype(bf16)
        for l in range(NL):
            for held, c in ((keep, me), (send, 1 - me)):
                block = weight_block(weights, 1 - which, l, c)
                total = lax.dot_general(
                    rows, block, (((1,), (1,)), ((), ())), preferred_element_type=f32
                )
                held[:, l, which] = total.astype(bf16).reshape(NX, ROWS, 2 * ROWS)


def call(kernel, inputs, out_shape, flops, scratch=(), first_smem=True):
    specs = [VMEM] * len(inputs)
    if first_smem:
        specs[0] = SMEM
    many = isinstance(out_shape, tuple)
    return pl.pallas_call(
        kernel,
        out_shape=out_shape,
        in_specs=specs,
        out_specs=(VMEM,) * len(out_shape) if many else VMEM,
        scratch_shapes=list(scratch),
        compiler_params=PARAMS,
        cost_estimate=pl.CostEstimate(
            flops=flops,
            bytes_accessed=sum(a.size * a.dtype.itemsize for a in inputs),
            transcendentals=0,
        ),
    )(*inputs)


def on_device(tokens, gate_values, filters, input_weight, output_weight, cotangent):
    tokens_here, features = tokens.shape
    channels = gate_values.shape[1]
    me = lax.axis_index("core").astype(jnp.int32).reshape(1)
    swap = swap_pairs()

    pair, rows = lax.optimization_barrier(
        (jnp.stack([input_weight, output_weight.T]), jnp.stack([tokens, cotangent]))
    )
    weights = lax.all_gather(pair, "y", axis=0)
    moved = lax.ppermute(rows, ALL, swap)
    copies = jnp.broadcast_to(moved[None], (NH * NL, 2, tokens_here, features))
    own = lax.all_to_all(copies, Z, split_axis=0, concat_axis=0, tiled=True)
    own, weights = lax.optimization_barrier((own, weights))
    other = lax.ppermute(own, "core", [(0, 1), (1, 0)])
    held = (NH, NL, 2, tokens_here, features)
    own, other = own.reshape(held), other.reshape(held)

    half = NX * ROWS
    sent = call(
        project_kernel,
        (me, own, other, weights, filters, gate_values),
        jax.ShapeDtypeStruct((channels, 2 * half + 2 * ROWS), bf16),
        4 * half * 1024 * channels,
    )
    got = lax.all_to_all(
        sent.reshape(BLOCKS, OWN, 2 * half + 2 * ROWS), CTX, split_axis=0, concat_axis=0, tiled=True
    )
    per_channel = pltpu.VMEM((BLOCKS * OWN, ROWS), f32)
    sent = call(
        convolve_kernel,
        (got,) + tables(),
        jax.ShapeDtypeStruct((BLOCKS, OWN, 2 * half + ROWS), bf16),
        2 * 40 * OWN * FREQS * 256 * 256,
        [per_channel] * 4
        + [
            pltpu.VMEM((3 * OWN * FREQS, 2 * ROWS), bf16),
            pltpu.VMEM((3 * OWN * FREQS, 2 * ROWS), f32),
            pltpu.VMEM((2 * OWN * FREQS, 2 * ROWS), bf16),
            pltpu.VMEM((2 * OWN * FREQS, 2 * ROWS), f32),
        ]
        + [per_channel] * 3,
        first_smem=False,
    )
    got = lax.all_to_all(sent, CTX, split_axis=0, concat_axis=0, tiled=True)
    got = got.reshape(channels, 2 * half + ROWS)
    streams, grad_gate = got[:, : 2 * half], got[:, 2 * half :].T

    grads = call(
        weight_grad_kernel,
        (me, streams, own, other),
        jax.ShapeDtypeStruct((NY, 2, channels, ROWS), bf16),
        4 * half * 1024 * channels,
    )
    grads = lax.psum_scatter(grads, "y", scatter_dimension=0, tiled=True)
    grad_input_weight, grad_output_weight = grads[0, 0].T, grads[0, 1]

    shape = jax.ShapeDtypeStruct(held, bf16)
    keep, send = call(
        output_kernel, (me, streams, weights), (shape, shape), 4 * half * 1024 * channels
    )
    arrived = lax.ppermute(send, "core", [(0, 1), (1, 0)])
    parts = (keep.astype(f32) + arrived.astype(f32)).astype(bf16)
    parts = lax.all_to_all(
        parts.reshape(NH * NL, 2, tokens_here, features), Z, split_axis=0, concat_axis=0, tiled=True
    )
    total = jnp.sum(parts.astype(f32), 0).astype(bf16)
    total = lax.ppermute(total, ALL, swap)
    return (total[0], total[1], grad_gate, grad_input_weight, grad_output_weight)


def solution(mesh):
    chips = Mesh(mesh.devices.reshape(NX, NY, NH, NL, NC), ALL)
    rows, columns = P(CTX, TP), P(TP, CTX)
    return jax.shard_map(
        on_device,
        mesh=chips,
        in_specs=(rows, rows, rows, rows, columns, rows),
        out_specs=(rows, rows, rows, rows, columns),
        check_vma=False,
    )
```

```python
import math

import jax
import jax.numpy as jnp
import numpy as np
from jax import lax
from jax.experimental import pallas as pl
from jax.experimental.pallas import tpu as pltpu
from jax.sharding import Mesh, PartitionSpec as P

bf16 = jnp.bfloat16
f32 = jnp.float32

NX, NY, NH, NL, NC = 4, 8, 4, 2, 2
CTX = ("x", "y")
TP = ("zh", "zl", "core")
ALL = CTX + TP
Z = ("zh", "zl")

BLOCKS = NX * NY
ROWS = 128
FREQS = 2 * BLOCKS
LENGTH = FREQS * ROWS
SPARE = 16
OWN = 8

VMEM = pl.BlockSpec(memory_space=pltpu.VMEM)
SMEM = pl.BlockSpec(memory_space=pltpu.SMEM)
PARAMS = pltpu.CompilerParams(vmem_limit_bytes=48 * 1024 * 1024)


def swap_pairs():
    def place(x, y, h, l, c):
        return (((x * NY + y) * NH + h) * NL + l) * NC + c

    return [
        (place(x, y, h, l, c), place(h, y, x, l, c))
        for x in range(NX)
        for y in range(NY)
        for h in range(NH)
        for l in range(NL)
        for c in range(NC)
    ]


def tables():
    freq = np.arange(FREQS)
    block = np.arange(BLOCKS)
    row = np.arange(ROWS)
    angle = 2 * math.pi * (freq[:, None] * block[None, :] % FREQS) / FREQS
    first = np.concatenate([np.cos(angle), -np.sin(angle)], 0)
    twist = 2 * math.pi * (freq[:, None] * row[None, :] % LENGTH) / LENGTH
    angle = 2 * math.pi * (row[:, None] * row[None, :] % ROWS) / ROWS
    cosine, sine = np.cos(angle), np.sin(angle)
    second = np.block([[cosine, -sine], [sine, cosine]])
    return (
        jnp.asarray(first, bf16),
        jnp.asarray(first.T, bf16),
        jnp.asarray(np.cos(twist), f32),
        jnp.asarray(np.sin(twist), f32),
        jnp.asarray(second, bf16),
        jnp.asarray(second.T, bf16),
    )


def dot(left, right):
    return jnp.dot(left, right, preferred_element_type=f32)


def weight_block(weights, which, l, c):
    first = 4 * l + 2 * c
    return jnp.concatenate([weights[first, which, :ROWS], weights[first + 1, which, :ROWS]], 0)


def product_terms(held, weights, which, c):
    total = None
    for l in range(NL):
        rows = held[:, l, which].reshape(NX * ROWS, 2 * ROWS)
        term = dot(rows, weight_block(weights, which, l, c))
        total = term if total is None else total + term
    return total


def project_own_kernel(me_ref, own, weights, totals):
    for which in range(2):
        totals[which] = product_terms(own, weights, which, me_ref[0])


def project_kernel(me_ref, other, weights, totals, filters, gate, out):
    for which in range(2):
        total = totals[which] + product_terms(other, weights, which, 1 - me_ref[0])
        out[:, which * NX * ROWS : (which + 1) * NX * ROWS] = total.T.astype(bf16)
    base = 2 * NX * ROWS
    out[:, base : base + ROWS] = filters[...].astype(f32).T.astype(bf16)
    out[:, base + ROWS : base + 2 * ROWS] = gate[...].astype(f32).T.astype(bf16)


def convolve_kernel(
    got, first, first_back, twist_cos, twist_sin, second, second_back, out,
    proj, gmod, filt, gate, mixed, spectrum, product, back, o_mod, o_gp, o_gg,
):
    half = NX * ROWS

    def lanes(start):
        return slice(start, start + ROWS)

    for y in range(NY):
        for x in range(NX):
            b = x * NY + y
            at = slice(b * OWN, (b + 1) * OWN)
            for base, held in ((0, proj), (half, gmod)):
                total = got[y, :, lanes(base + x * ROWS)].astype(f32)
                for k in range(1, NX):
                    total = total + got[k * NY + y, :, lanes(base + x * ROWS)].astype(f32)
                held[at, :] = total
            filt[at, :] = got[b, :, lanes(2 * half)].astype(f32)
            gate[at, :] = got[b, :, lanes(2 * half + ROWS)].astype(f32)
    cosine, sine = twist_cos[...], twist_sin[...]
    for c in range(OWN):
        pick = pl.ds(c, BLOCKS, stride=OWN)
        signals = jnp.concatenate(
            [
                proj[pick, :].astype(bf16),
                (gmod[pick, :] * gate[pick, :]).astype(bf16),
                filt[pick, :].astype(bf16),
            ],
            1,
        )
        parts = dot(first[...], signals)
        for i in range(3):
            real = parts[:FREQS, lanes(i * ROWS)]
            imag = parts[FREQS:, lanes(i * ROWS)]
            at = slice((c * 3 + i) * FREQS, (c * 3 + i + 1) * FREQS)
            mixed[at, :ROWS] = (real * cosine + imag * sine).astype(bf16)
            mixed[at, ROWS:] = (imag * cosine - real * sine).astype(bf16)
    spectrum[...] = dot(mixed[...], second[...])
    for c in range(OWN):
        (xr, xi), (gr, gi), (hr, hi) = [
            (spectrum[at, :ROWS], spectrum[at, ROWS:])
            for at in [slice((c * 3 + i) * FREQS, (c * 3 + i + 1) * FREQS) for i in range(3)]
        ]
        at = slice(2 * c * FREQS, (2 * c + 1) * FREQS)
        product[at, :ROWS] = (xr * hr - xi * hi).astype(bf16)
        product[at, ROWS:] = (xr * hi + xi * hr).astype(bf16)
        at = slice((2 * c + 1) * FREQS, (2 * c + 2) * FREQS)
        product[at, :ROWS] = (gr * hr + gi * hi).astype(bf16)
        product[at, ROWS:] = (gi * hr - gr * hi).astype(bf16)
    back[...] = dot(product[...], second_back[...])
    for c in range(OWN):
        pick = pl.ds(c, BLOCKS, stride=OWN)
        columns = []
        for i in range(2):
            at = slice((2 * c + i) * FREQS, (2 * c + i + 1) * FREQS)
            real, imag = back[at, :ROWS], back[at, ROWS:]
            columns.append(
                jnp.concatenate(
                    [
                        (real * cosine - imag * sine).astype(bf16),
                        (imag * cosine + real * sine).astype(bf16),
                    ],
                    0,
                )
            )
        in_time = dot(first_back[...], jnp.concatenate(columns, 1)) * (1.0 / LENGTH)
        convolved = in_time[:, :ROWS]
        o_gp[pick, :] = in_time[:, ROWS:]
        o_mod[pick, :] = gate[pick, :] * convolved
        o_gg[pick, :] = gmod[pick, :] * convolved
    for y in range(NY):
        for x in range(NX):
            b = x * NY + y
            at = slice(b * OWN, (b + 1) * OWN)
            modulated = o_mod[at, :].astype(bf16)
            grad = o_gp[at, :].astype(bf16)
            for k in range(NX):
                out[k * NY + y, :, lanes(x * ROWS)] = modulated
                out[k * NY + y, :, lanes(half + x * ROWS)] = grad
            out[b, :, lanes(2 * half)] = o_gg[at, :].astype(bf16)


def weight_grad_kernel(me_ref, got, own, other, out):
    me = me_ref[0]
    half = NX * ROWS
    for which in range(2):
        left = got[:, half:] if which == 0 else got[:, :half]
        for l in range(NL):
            for held, c in ((own, me), (other, 1 - me)):
                rows = held[:, l, which].reshape(half, 2 * ROWS)
                total = dot(left, rows).astype(bf16)
                out[4 * l + 2 * c, which] = total[:, :ROWS]
                out[4 * l + 2 * c + 1, which] = total[:, ROWS:]


def output_kernel(me_ref, got, weights, keep, send):
    me = me_ref[0]
    half = NX * ROWS
    for which in range(2):
        start = which * half
        rows = got[:, start : start + half].astype(f32).T.astype(bf16)
        for l in range(NL):
            for held, c in ((keep, me), (send, 1 - me)):
                block = weight_block(weights, 1 - which, l, c)
                total = lax.dot_general(
                    rows, block, (((1,), (1,)), ((), ())), preferred_element_type=f32
                )
                held[:, l, which] = total.astype(bf16).reshape(NX, ROWS, 2 * ROWS)


def call(kernel, inputs, out_shape, flops, scratch=(), first_smem=True):
    specs = [VMEM] * len(inputs)
    if first_smem:
        specs[0] = SMEM
    many = isinstance(out_shape, tuple)
    return pl.pallas_call(
        kernel,
        out_shape=out_shape,
        in_specs=specs,
        out_specs=(VMEM,) * len(out_shape) if many else VMEM,
        scratch_shapes=list(scratch),
        compiler_params=PARAMS,
        cost_estimate=pl.CostEstimate(
            flops=flops,
            bytes_accessed=sum(a.size * a.dtype.itemsize for a in inputs),
            transcendentals=0,
        ),
    )(*inputs)


def on_device(tokens, gate_values, filters, input_weight, output_weight, cotangent):
    tokens_here, features = tokens.shape
    channels = gate_values.shape[1]
    me = lax.axis_index("core").astype(jnp.int32).reshape(1)
    swap = swap_pairs()

    pair, rows = lax.optimization_barrier(
        (jnp.stack([input_weight, output_weight.T]), jnp.stack([tokens, cotangent]))
    )
    weights = lax.all_gather(jnp.pad(pair, ((0, 0), (0, SPARE), (0, 0))), "y", axis=0)
    moved = lax.ppermute(rows, ALL, swap)
    copies = jnp.broadcast_to(moved[None], (NH * NL, 2, tokens_here, features))
    own = lax.all_to_all(copies, Z, split_axis=0, concat_axis=0, tiled=True)
    other = lax.ppermute(own, "core", [(0, 1), (1, 0)])
    held = (NH, NL, 2, tokens_here, features)
    own, other = own.reshape(held), other.reshape(held)

    half = NX * ROWS
    totals = call(
        project_own_kernel,
        (me, own, weights),
        jax.ShapeDtypeStruct((2, half, channels), f32),
        4 * half * 512 * channels,
    )
    sent = call(
        project_kernel,
        (me, other, weights, totals, filters, gate_values),
        jax.ShapeDtypeStruct((channels, 2 * half + 2 * ROWS), bf16),
        4 * half * 512 * channels,
    )
    got = lax.all_to_all(
        sent.reshape(BLOCKS, OWN, 2 * half + 2 * ROWS), CTX, split_axis=0, concat_axis=0, tiled=True
    )
    per_channel = pltpu.VMEM((BLOCKS * OWN, ROWS), f32)
    sent = call(
        convolve_kernel,
        (got,) + tables(),
        jax.ShapeDtypeStruct((BLOCKS, OWN, 2 * half + ROWS), bf16),
        2 * 40 * OWN * FREQS * 256 * 256,
        [per_channel] * 4
        + [
            pltpu.VMEM((3 * OWN * FREQS, 2 * ROWS), bf16),
            pltpu.VMEM((3 * OWN * FREQS, 2 * ROWS), f32),
            pltpu.VMEM((2 * OWN * FREQS, 2 * ROWS), bf16),
            pltpu.VMEM((2 * OWN * FREQS, 2 * ROWS), f32),
        ]
        + [per_channel] * 3,
        first_smem=False,
    )
    got = lax.all_to_all(sent, CTX, split_axis=0, concat_axis=0, tiled=True)
    got = got.reshape(channels, 2 * half + ROWS)
    streams, grad_gate = got[:, : 2 * half], got[:, 2 * half :].T

    grads = call(
        weight_grad_kernel,
        (me, streams, own, other),
        jax.ShapeDtypeStruct((NY, 2, channels, ROWS), bf16),
        4 * half * 1024 * channels,
    )
    grads = lax.psum_scatter(grads, "y", scatter_dimension=0, tiled=True)
    grad_input_weight, grad_output_weight = grads[0, 0].T, grads[0, 1]

    shape = jax.ShapeDtypeStruct(held, bf16)
    keep, send = call(
        output_kernel, (me, streams, weights), (shape, shape), 4 * half * 1024 * channels
    )
    arrived = lax.ppermute(send, "core", [(0, 1), (1, 0)])
    parts = (keep.astype(f32) + arrived.astype(f32)).astype(bf16)
    parts = lax.all_to_all(
        parts.reshape(NH * NL, 2, tokens_here, features), Z, split_axis=0, concat_axis=0, tiled=True
    )
    total = jnp.sum(parts.astype(f32), 0).astype(bf16)
    total = lax.ppermute(total, ALL, swap)
    return (total[0], total[1], grad_gate, grad_input_weight, grad_output_weight)


def solution(mesh):
    chips = Mesh(mesh.devices.reshape(NX, NY, NH, NL, NC), ALL)
    rows, columns = P(CTX, TP), P(TP, CTX)
    return jax.shard_map(
        on_device,
        mesh=chips,
        in_specs=(rows, rows, rows, rows, columns, rows),
        out_specs=(rows, rows, rows, rows, columns),
        check_vma=False,
    )
```

```python
import math

import jax
import jax.numpy as jnp
import numpy as np
from jax import lax
from jax.experimental import pallas as pl
from jax.experimental.pallas import tpu as pltpu
from jax.sharding import Mesh, PartitionSpec as P

bf16 = jnp.bfloat16
f32 = jnp.float32

NX, NY, NH, NL, NC = 4, 8, 4, 2, 2
CTX = ("x", "y")
TP = ("zh", "zl", "core")
ALL = CTX + TP
Z = ("zh", "zl")

BLOCKS = NX * NY
ROWS = 128
FREQS = 2 * BLOCKS
LENGTH = FREQS * ROWS
SPARE = 16
OWN = 8

VMEM = pl.BlockSpec(memory_space=pltpu.VMEM)
SMEM = pl.BlockSpec(memory_space=pltpu.SMEM)
PARAMS = pltpu.CompilerParams(vmem_limit_bytes=48 * 1024 * 1024)


def swap_pairs():
    def place(x, y, h, l, c):
        return (((x * NY + y) * NH + h) * NL + l) * NC + c

    return [
        (place(x, y, h, l, c), place(h, y, x, l, c))
        for x in range(NX)
        for y in range(NY)
        for h in range(NH)
        for l in range(NL)
        for c in range(NC)
    ]


def tables():
    freq = np.arange(FREQS)
    block = np.arange(BLOCKS)
    row = np.arange(ROWS)
    angle = 2 * math.pi * (freq[:, None] * block[None, :] % FREQS) / FREQS
    first = np.concatenate([np.cos(angle), -np.sin(angle)], 0)
    twist = 2 * math.pi * (freq[:, None] * row[None, :] % LENGTH) / LENGTH
    angle = 2 * math.pi * (row[:, None] * row[None, :] % ROWS) / ROWS
    cosine, sine = np.cos(angle), np.sin(angle)
    second = np.block([[cosine, -sine], [sine, cosine]])
    return (
        jnp.asarray(first, bf16),
        jnp.asarray(first.T, bf16),
        jnp.asarray(np.cos(twist), f32),
        jnp.asarray(np.sin(twist), f32),
        jnp.asarray(second, bf16),
        jnp.asarray(second.T, bf16),
    )


def dot(left, right):
    return jnp.dot(left, right, preferred_element_type=f32)


def weight_block(weights, which, l, c):
    first = 4 * l + 2 * c
    return jnp.concatenate([weights[first, which, :ROWS], weights[first + 1, which, :ROWS]], 0)


def product_terms(held, weights, which, c):
    total = None
    for l in range(NL):
        rows = held[:, l, which].reshape(NX * ROWS, 2 * ROWS)
        term = dot(rows, weight_block(weights, which, l, c))
        total = term if total is None else total + term
    return total


def project_own_kernel(me_ref, own, weights, totals):
    for which in range(2):
        totals[which] = product_terms(own, weights, which, me_ref[0])


def project_kernel(me_ref, other, weights, totals, filters, gate, out):
    for which in range(2):
        total = totals[which] + product_terms(other, weights, which, 1 - me_ref[0])
        out[:, which * NX * ROWS : (which + 1) * NX * ROWS] = total.T.astype(bf16)
    base = 2 * NX * ROWS
    out[:, base : base + ROWS] = filters[...].astype(f32).T.astype(bf16)
    out[:, base + ROWS : base + 2 * ROWS] = gate[...].astype(f32).T.astype(bf16)


def convolve_kernel(
    got, first, first_back, twist_cos, twist_sin, second, second_back, out,
    proj, gmod, filt, gate, mixed, spectrum, product, back, o_mod, o_gp, o_gg,
):
    half = NX * ROWS

    def lanes(start):
        return slice(start, start + ROWS)

    for y in range(NY):
        for x in range(NX):
            b = x * NY + y
            at = slice(b * OWN, (b + 1) * OWN)
            for base, held in ((0, proj), (half, gmod)):
                total = got[y, :, lanes(base + x * ROWS)].astype(f32)
                for k in range(1, NX):
                    total = total + got[k * NY + y, :, lanes(base + x * ROWS)].astype(f32)
                held[at, :] = total
            filt[at, :] = got[b, :, lanes(2 * half)].astype(f32)
            gate[at, :] = got[b, :, lanes(2 * half + ROWS)].astype(f32)
    cosine, sine = twist_cos[...], twist_sin[...]
    for c in range(OWN):
        pick = pl.ds(c, BLOCKS, stride=OWN)
        signals = jnp.concatenate(
            [
                proj[pick, :].astype(bf16),
                (gmod[pick, :] * gate[pick, :]).astype(bf16),
                filt[pick, :].astype(bf16),
            ],
            1,
        )
        parts = dot(first[...], signals)
        for i in range(3):
            real = parts[:FREQS, lanes(i * ROWS)]
            imag = parts[FREQS:, lanes(i * ROWS)]
            at = slice((c * 3 + i) * FREQS, (c * 3 + i + 1) * FREQS)
            mixed[at, :ROWS] = (real * cosine + imag * sine).astype(bf16)
            mixed[at, ROWS:] = (imag * cosine - real * sine).astype(bf16)
    spectrum[...] = dot(mixed[...], second[...])
    for c in range(OWN):
        (xr, xi), (gr, gi), (hr, hi) = [
            (spectrum[at, :ROWS], spectrum[at, ROWS:])
            for at in [slice((c * 3 + i) * FREQS, (c * 3 + i + 1) * FREQS) for i in range(3)]
        ]
        at = slice(2 * c * FREQS, (2 * c + 1) * FREQS)
        product[at, :ROWS] = (xr * hr - xi * hi).astype(bf16)
        product[at, ROWS:] = (xr * hi + xi * hr).astype(bf16)
        at = slice((2 * c + 1) * FREQS, (2 * c + 2) * FREQS)
        product[at, :ROWS] = (gr * hr + gi * hi).astype(bf16)
        product[at, ROWS:] = (gi * hr - gr * hi).astype(bf16)
    back[...] = dot(product[...], second_back[...])
    for c in range(OWN):
        pick = pl.ds(c, BLOCKS, stride=OWN)
        columns = []
        for i in range(2):
            at = slice((2 * c + i) * FREQS, (2 * c + i + 1) * FREQS)
            real, imag = back[at, :ROWS], back[at, ROWS:]
            columns.append(
                jnp.concatenate(
                    [
                        (real * cosine - imag * sine).astype(bf16),
                        (imag * cosine + real * sine).astype(bf16),
                    ],
                    0,
                )
            )
        in_time = dot(first_back[...], jnp.concatenate(columns, 1)) * (1.0 / LENGTH)
        convolved = in_time[:, :ROWS]
        o_gp[pick, :] = in_time[:, ROWS:]
        o_mod[pick, :] = gate[pick, :] * convolved
        o_gg[pick, :] = gmod[pick, :] * convolved
    for y in range(NY):
        for x in range(NX):
            b = x * NY + y
            at = slice(b * OWN, (b + 1) * OWN)
            modulated = o_mod[at, :].astype(bf16)
            grad = o_gp[at, :].astype(bf16)
            for k in range(NX):
                out[k * NY + y, :, lanes(x * ROWS)] = modulated
                out[k * NY + y, :, lanes(half + x * ROWS)] = grad
            out[b, :, lanes(2 * half)] = o_gg[at, :].astype(bf16)


def weight_grad_kernel(me_ref, got, own, other, out):
    me = me_ref[0]
    half = NX * ROWS
    for which in range(2):
        left = got[:, half:] if which == 0 else got[:, :half]
        for l in range(NL):
            for held, c in ((own, me), (other, 1 - me)):
                rows = held[:, l, which].reshape(half, 2 * ROWS)
                total = dot(left, rows).astype(bf16)
                out[4 * l + 2 * c, which] = total[:, :ROWS]
                out[4 * l + 2 * c + 1, which] = total[:, ROWS:]


def output_kernel(me_ref, got, weights, keep, send):
    me = me_ref[0]
    half = NX * ROWS
    for which in range(2):
        start = which * half
        rows = got[:, start : start + half].astype(f32).T.astype(bf16)
        for l in range(NL):
            for held, c in ((keep, me), (send, 1 - me)):
                block = weight_block(weights, 1 - which, l, c)
                total = lax.dot_general(
                    rows, block, (((1,), (1,)), ((), ())), preferred_element_type=f32
                )
                held[:, l, which] = total.astype(bf16).reshape(NX, ROWS, 2 * ROWS)


def call(kernel, inputs, out_shape, flops, scratch=(), first_smem=True):
    specs = [VMEM] * len(inputs)
    if first_smem:
        specs[0] = SMEM
    many = isinstance(out_shape, tuple)
    return pl.pallas_call(
        kernel,
        out_shape=out_shape,
        in_specs=specs,
        out_specs=(VMEM,) * len(out_shape) if many else VMEM,
        scratch_shapes=list(scratch),
        compiler_params=PARAMS,
        cost_estimate=pl.CostEstimate(
            flops=flops,
            bytes_accessed=sum(a.size * a.dtype.itemsize for a in inputs),
            transcendentals=0,
        ),
    )(*inputs)


def on_device(tokens, gate_values, filters, input_weight, output_weight, cotangent):
    tokens_here, features = tokens.shape
    channels = gate_values.shape[1]
    me = lax.axis_index("core").astype(jnp.int32).reshape(1)
    swap = swap_pairs()

    pair, rows = lax.optimization_barrier(
        (
            jnp.pad(jnp.stack([input_weight, output_weight.T]), ((0, 0), (0, SPARE), (0, 0))),
            jnp.stack([tokens, cotangent]),
        )
    )
    weights = lax.all_gather(pair, "y", axis=0)
    moved = lax.ppermute(rows, ALL, swap)
    copies = jnp.broadcast_to(moved[None], (NH * NL, 2, tokens_here, features))
    own = lax.all_to_all(copies, Z, split_axis=0, concat_axis=0, tiled=True)
    other = lax.ppermute(own, "core", [(0, 1), (1, 0)])
    held = (NH, NL, 2, tokens_here, features)
    own, other = own.reshape(held), other.reshape(held)

    half = NX * ROWS
    totals = call(
        project_own_kernel,
        (me, own, weights),
        jax.ShapeDtypeStruct((2, half, channels), f32),
        160 * half * 512 * channels,
    )
    sent = call(
        project_kernel,
        (me, other, weights, totals, filters, gate_values),
        jax.ShapeDtypeStruct((channels, 2 * half + 2 * ROWS), bf16),
        4 * half * 512 * channels,
    )
    got = lax.all_to_all(
        sent.reshape(BLOCKS, OWN, 2 * half + 2 * ROWS), CTX, split_axis=0, concat_axis=0, tiled=True
    )
    per_channel = pltpu.VMEM((BLOCKS * OWN, ROWS), f32)
    sent = call(
        convolve_kernel,
        (got,) + tables(),
        jax.ShapeDtypeStruct((BLOCKS, OWN, 2 * half + ROWS), bf16),
        2 * 40 * OWN * FREQS * 256 * 256,
        [per_channel] * 4
        + [
            pltpu.VMEM((3 * OWN * FREQS, 2 * ROWS), bf16),
            pltpu.VMEM((3 * OWN * FREQS, 2 * ROWS), f32),
            pltpu.VMEM((2 * OWN * FREQS, 2 * ROWS), bf16),
            pltpu.VMEM((2 * OWN * FREQS, 2 * ROWS), f32),
        ]
        + [per_channel] * 3,
        first_smem=False,
    )
    got = lax.all_to_all(sent, CTX, split_axis=0, concat_axis=0, tiled=True)
    got = got.reshape(channels, 2 * half + ROWS)
    streams, grad_gate = got[:, : 2 * half], got[:, 2 * half :].T

    grads = call(
        weight_grad_kernel,
        (me, streams, own, other),
        jax.ShapeDtypeStruct((NY, 2, channels, ROWS), bf16),
        4 * half * 1024 * channels,
    )
    grads = lax.psum_scatter(grads, "y", scatter_dimension=0, tiled=True)
    grad_input_weight, grad_output_weight = grads[0, 0].T, grads[0, 1]

    shape = jax.ShapeDtypeStruct(held, bf16)
    keep, send = call(
        output_kernel, (me, streams, weights), (shape, shape), 4 * half * 1024 * channels
    )
    arrived = lax.ppermute(send, "core", [(0, 1), (1, 0)])
    parts = (keep.astype(f32) + arrived.astype(f32)).astype(bf16)
    parts = lax.all_to_all(
        parts.reshape(NH * NL, 2, tokens_here, features), Z, split_axis=0, concat_axis=0, tiled=True
    )
    total = jnp.sum(parts.astype(f32), 0).astype(bf16)
    total = lax.ppermute(total, ALL, swap)
    return (total[0], total[1], grad_gate, grad_input_weight, grad_output_weight)


def solution(mesh):
    chips = Mesh(mesh.devices.reshape(NX, NY, NH, NL, NC), ALL)
    rows, columns = P(CTX, TP), P(TP, CTX)
    return jax.shard_map(
        on_device,
        mesh=chips,
        in_specs=(rows, rows, rows, rows, columns, rows),
        out_specs=(rows, rows, rows, rows, columns),
        check_vma=False,
    )
```

```python
import math

import jax
import jax.numpy as jnp
import numpy as np
from jax import lax
from jax.experimental import pallas as pl
from jax.experimental.pallas import tpu as pltpu
from jax.sharding import Mesh, PartitionSpec as P

bf16 = jnp.bfloat16
f32 = jnp.float32

NX, NY, NH, NL, NC = 4, 8, 4, 2, 2
CTX = ("x", "y")
TP = ("zh", "zl", "core")
ALL = CTX + TP
Z = ("zh", "zl")

BLOCKS = NX * NY
ROWS = 128
FREQS = 2 * BLOCKS
LENGTH = FREQS * ROWS
SPARE = 8
OWN = 8

VMEM = pl.BlockSpec(memory_space=pltpu.VMEM)
SMEM = pl.BlockSpec(memory_space=pltpu.SMEM)
PARAMS = pltpu.CompilerParams(vmem_limit_bytes=48 * 1024 * 1024)


def swap_pairs():
    def place(x, y, h, l, c):
        return (((x * NY + y) * NH + h) * NL + l) * NC + c

    return [
        (place(x, y, h, l, c), place(h, y, x, l, c))
        for x in range(NX)
        for y in range(NY)
        for h in range(NH)
        for l in range(NL)
        for c in range(NC)
    ]


def tables():
    freq = np.arange(FREQS)
    block = np.arange(BLOCKS)
    row = np.arange(ROWS)
    angle = 2 * math.pi * (freq[:, None] * block[None, :] % FREQS) / FREQS
    first = np.concatenate([np.cos(angle), -np.sin(angle)], 0)
    twist = 2 * math.pi * (freq[:, None] * row[None, :] % LENGTH) / LENGTH
    angle = 2 * math.pi * (row[:, None] * row[None, :] % ROWS) / ROWS
    cosine, sine = np.cos(angle), np.sin(angle)
    second = np.block([[cosine, -sine], [sine, cosine]])
    return (
        jnp.asarray(first, bf16),
        jnp.asarray(first.T, bf16),
        jnp.asarray(np.cos(twist), f32),
        jnp.asarray(np.sin(twist), f32),
        jnp.asarray(second, bf16),
        jnp.asarray(second.T, bf16),
    )


def dot(left, right):
    return jnp.dot(left, right, preferred_element_type=f32)


def weight_block(weights, which, l, c):
    first = 4 * l + 2 * c
    return jnp.concatenate([weights[first, which, :ROWS], weights[first + 1, which, :ROWS]], 0)


def product_terms(held, weights, which, c):
    total = None
    for l in range(NL):
        rows = held[:, l, which].reshape(NX * ROWS, 2 * ROWS)
        term = dot(rows, weight_block(weights, which, l, c))
        total = term if total is None else total + term
    return total


def project_own_kernel(me_ref, own, weights, totals):
    for which in range(2):
        totals[which] = product_terms(own, weights, which, me_ref[0])


def project_kernel(me_ref, other, weights, totals, filters, gate, out):
    for which in range(2):
        total = totals[which] + product_terms(other, weights, which, 1 - me_ref[0])
        out[:, which * NX * ROWS : (which + 1) * NX * ROWS] = total.T.astype(bf16)
    base = 2 * NX * ROWS
    out[:, base : base + ROWS] = filters[...].astype(f32).T.astype(bf16)
    out[:, base + ROWS : base + 2 * ROWS] = gate[...].astype(f32).T.astype(bf16)


def convolve_kernel(
    got, first, first_back, twist_cos, twist_sin, second, second_back, out,
    proj, gmod, filt, gate, mixed, spectrum, product, back, o_mod, o_gp, o_gg,
):
    half = NX * ROWS

    def lanes(start):
        return slice(start, start + ROWS)

    for y in range(NY):
        for x in range(NX):
            b = x * NY + y
            at = slice(b * OWN, (b + 1) * OWN)
            for base, held in ((0, proj), (half, gmod)):
                total = got[y, :, lanes(base + x * ROWS)].astype(f32)
                for k in range(1, NX):
                    total = total + got[k * NY + y, :, lanes(base + x * ROWS)].astype(f32)
                held[at, :] = total
            filt[at, :] = got[b, :, lanes(2 * half)].astype(f32)
            gate[at, :] = got[b, :, lanes(2 * half + ROWS)].astype(f32)
    cosine, sine = twist_cos[...], twist_sin[...]
    for c in range(OWN):
        pick = pl.ds(c, BLOCKS, stride=OWN)
        signals = jnp.concatenate(
            [
                proj[pick, :].astype(bf16),
                (gmod[pick, :] * gate[pick, :]).astype(bf16),
                filt[pick, :].astype(bf16),
            ],
            1,
        )
        parts = dot(first[...], signals)
        for i in range(3):
            real = parts[:FREQS, lanes(i * ROWS)]
            imag = parts[FREQS:, lanes(i * ROWS)]
            at = slice((c * 3 + i) * FREQS, (c * 3 + i + 1) * FREQS)
            mixed[at, :ROWS] = (real * cosine + imag * sine).astype(bf16)
            mixed[at, ROWS:] = (imag * cosine - real * sine).astype(bf16)
    spectrum[...] = dot(mixed[...], second[...])
    for c in range(OWN):
        (xr, xi), (gr, gi), (hr, hi) = [
            (spectrum[at, :ROWS], spectrum[at, ROWS:])
            for at in [slice((c * 3 + i) * FREQS, (c * 3 + i + 1) * FREQS) for i in range(3)]
        ]
        at = slice(2 * c * FREQS, (2 * c + 1) * FREQS)
        product[at, :ROWS] = (xr * hr - xi * hi).astype(bf16)
        product[at, ROWS:] = (xr * hi + xi * hr).astype(bf16)
        at = slice((2 * c + 1) * FREQS, (2 * c + 2) * FREQS)
        product[at, :ROWS] = (gr * hr + gi * hi).astype(bf16)
        product[at, ROWS:] = (gi * hr - gr * hi).astype(bf16)
    back[...] = dot(product[...], second_back[...])
    for c in range(OWN):
        pick = pl.ds(c, BLOCKS, stride=OWN)
        columns = []
        for i in range(2):
            at = slice((2 * c + i) * FREQS, (2 * c + i + 1) * FREQS)
            real, imag = back[at, :ROWS], back[at, ROWS:]
            columns.append(
                jnp.concatenate(
                    [
                        (real * cosine - imag * sine).astype(bf16),
                        (imag * cosine + real * sine).astype(bf16),
                    ],
                    0,
                )
            )
        in_time = dot(first_back[...], jnp.concatenate(columns, 1)) * (1.0 / LENGTH)
        convolved = in_time[:, :ROWS]
        o_gp[pick, :] = in_time[:, ROWS:]
        o_mod[pick, :] = gate[pick, :] * convolved
        o_gg[pick, :] = gmod[pick, :] * convolved
    for y in range(NY):
        for x in range(NX):
            b = x * NY + y
            at = slice(b * OWN, (b + 1) * OWN)
            modulated = o_mod[at, :].astype(bf16)
            grad = o_gp[at, :].astype(bf16)
            for k in range(NX):
                out[k * NY + y, :, lanes(x * ROWS)] = modulated
                out[k * NY + y, :, lanes(half + x * ROWS)] = grad
            out[b, :, lanes(2 * half)] = o_gg[at, :].astype(bf16)


def weight_grad_kernel(me_ref, got, own, other, out):
    me = me_ref[0]
    half = NX * ROWS
    for which in range(2):
        left = got[:, half:] if which == 0 else got[:, :half]
        for l in range(NL):
            for held, c in ((own, me), (other, 1 - me)):
                rows = held[:, l, which].reshape(half, 2 * ROWS)
                total = dot(left, rows).astype(bf16)
                out[4 * l + 2 * c, which] = total[:, :ROWS]
                out[4 * l + 2 * c + 1, which] = total[:, ROWS:]


def output_kernel(me_ref, got, weights, keep, send):
    me = me_ref[0]
    half = NX * ROWS
    for which in range(2):
        start = which * half
        rows = got[:, start : start + half].astype(f32).T.astype(bf16)
        for l in range(NL):
            for held, c in ((keep, me), (send, 1 - me)):
                block = weight_block(weights, 1 - which, l, c)
                total = lax.dot_general(
                    rows, block, (((1,), (1,)), ((), ())), preferred_element_type=f32
                )
                held[:, l, which] = total.astype(bf16).reshape(NX, ROWS, 2 * ROWS)


def call(kernel, inputs, out_shape, flops, scratch=(), first_smem=True):
    specs = [VMEM] * len(inputs)
    if first_smem:
        specs[0] = SMEM
    many = isinstance(out_shape, tuple)
    return pl.pallas_call(
        kernel,
        out_shape=out_shape,
        in_specs=specs,
        out_specs=(VMEM,) * len(out_shape) if many else VMEM,
        scratch_shapes=list(scratch),
        compiler_params=PARAMS,
        cost_estimate=pl.CostEstimate(
            flops=flops,
            bytes_accessed=sum(a.size * a.dtype.itemsize for a in inputs),
            transcendentals=0,
        ),
    )(*inputs)


def on_device(tokens, gate_values, filters, input_weight, output_weight, cotangent):
    tokens_here, features = tokens.shape
    channels = gate_values.shape[1]
    me = lax.axis_index("core").astype(jnp.int32).reshape(1)
    swap = swap_pairs()

    pair = jnp.pad(jnp.stack([input_weight, output_weight.T]), ((0, 0), (0, SPARE), (0, 0)))
    weights = lax.all_gather(pair, "y", axis=0)
    moved = lax.ppermute(jnp.stack([tokens, cotangent]), ALL, swap)
    copies = jnp.broadcast_to(moved[None], (NH * NL, 2, tokens_here, features))
    own = lax.all_to_all(copies, Z, split_axis=0, concat_axis=0, tiled=True)
    other = lax.ppermute(own, "core", [(0, 1), (1, 0)])
    held = (NH, NL, 2, tokens_here, features)
    own, other = own.reshape(held), other.reshape(held)

    half = NX * ROWS
    totals = call(
        project_own_kernel,
        (me, own, weights),
        jax.ShapeDtypeStruct((2, half, channels), f32),
        160 * half * 512 * channels,
    )
    sent = call(
        project_kernel,
        (me, other, weights, totals, filters, gate_values),
        jax.ShapeDtypeStruct((channels, 2 * half + 2 * ROWS), bf16),
        4 * half * 512 * channels,
    )
    got = lax.all_to_all(
        sent.reshape(BLOCKS, OWN, 2 * half + 2 * ROWS), CTX, split_axis=0, concat_axis=0, tiled=True
    )
    per_channel = pltpu.VMEM((BLOCKS * OWN, ROWS), f32)
    sent = call(
        convolve_kernel,
        (got,) + tables(),
        jax.ShapeDtypeStruct((BLOCKS, OWN, 2 * half + ROWS), bf16),
        2 * 40 * OWN * FREQS * 256 * 256,
        [per_channel] * 4
        + [
            pltpu.VMEM((3 * OWN * FREQS, 2 * ROWS), bf16),
            pltpu.VMEM((3 * OWN * FREQS, 2 * ROWS), f32),
            pltpu.VMEM((2 * OWN * FREQS, 2 * ROWS), bf16),
            pltpu.VMEM((2 * OWN * FREQS, 2 * ROWS), f32),
        ]
        + [per_channel] * 3,
        first_smem=False,
    )
    got = lax.all_to_all(sent, CTX, split_axis=0, concat_axis=0, tiled=True)
    got = got.reshape(channels, 2 * half + ROWS)
    streams, grad_gate = got[:, : 2 * half], got[:, 2 * half :].T

    grads = call(
        weight_grad_kernel,
        (me, streams, own, other),
        jax.ShapeDtypeStruct((NY, 2, channels, ROWS), bf16),
        4 * half * 1024 * channels,
    )
    grads = lax.psum_scatter(grads, "y", scatter_dimension=0, tiled=True)
    grad_input_weight, grad_output_weight = grads[0, 0].T, grads[0, 1]

    shape = jax.ShapeDtypeStruct(held, bf16)
    keep, send = call(
        output_kernel, (me, streams, weights), (shape, shape), 4 * half * 1024 * channels
    )
    arrived = lax.ppermute(send, "core", [(0, 1), (1, 0)])
    parts = (keep.astype(f32) + arrived.astype(f32)).astype(bf16)
    parts = lax.all_to_all(
        parts.reshape(NH * NL, 2, tokens_here, features), Z, split_axis=0, concat_axis=0, tiled=True
    )
    total = jnp.sum(parts.astype(f32), 0).astype(bf16)
    total = lax.ppermute(total, ALL, swap)
    return (total[0], total[1], grad_gate, grad_input_weight, grad_output_weight)


def solution(mesh):
    chips = Mesh(mesh.devices.reshape(NX, NY, NH, NL, NC), ALL)
    rows, columns = P(CTX, TP), P(TP, CTX)
    return jax.shard_map(
        on_device,
        mesh=chips,
        in_specs=(rows, rows, rows, rows, columns, rows),
        out_specs=(rows, rows, rows, rows, columns),
        check_vma=False,
    )
```

```python
import math

import jax
import jax.numpy as jnp
import numpy as np
from jax import lax
from jax.experimental import pallas as pl
from jax.experimental.pallas import tpu as pltpu
from jax.sharding import Mesh, PartitionSpec as P

bf16 = jnp.bfloat16
f32 = jnp.float32

NX, NY, NH, NL, NC = 4, 8, 4, 2, 2
CTX = ("x", "y")
TP = ("zh", "zl", "core")
ALL = CTX + TP
Z = ("zh", "zl")

BLOCKS = NX * NY
ROWS = 128
FREQS = 2 * BLOCKS
LENGTH = FREQS * ROWS
SPARE = 8
OWN = 8

VMEM = pl.BlockSpec(memory_space=pltpu.VMEM)
SMEM = pl.BlockSpec(memory_space=pltpu.SMEM)
PARAMS = pltpu.CompilerParams(vmem_limit_bytes=48 * 1024 * 1024)


def swap_pairs():
    def place(x, y, h, l, c):
        return (((x * NY + y) * NH + h) * NL + l) * NC + c

    return [
        (place(x, y, h, l, c), place(h, y, x, l, c))
        for x in range(NX)
        for y in range(NY)
        for h in range(NH)
        for l in range(NL)
        for c in range(NC)
    ]


def tables():
    freq = np.arange(FREQS)
    block = np.arange(BLOCKS)
    row = np.arange(ROWS)
    angle = 2 * math.pi * (freq[:, None] * block[None, :] % FREQS) / FREQS
    first = np.concatenate([np.cos(angle), -np.sin(angle)], 0)
    twist = 2 * math.pi * (freq[:, None] * row[None, :] % LENGTH) / LENGTH
    angle = 2 * math.pi * (row[:, None] * row[None, :] % ROWS) / ROWS
    cosine, sine = np.cos(angle), np.sin(angle)
    second = np.block([[cosine, -sine], [sine, cosine]])
    return (
        jnp.asarray(first, bf16),
        jnp.asarray(first.T, bf16),
        jnp.asarray(np.cos(twist), f32),
        jnp.asarray(np.sin(twist), f32),
        jnp.asarray(second, bf16),
        jnp.asarray(second.T, bf16),
    )


def dot(left, right):
    return jnp.dot(left, right, preferred_element_type=f32)


def weight_block(weights, which, l, c):
    first = 4 * l + 2 * c
    return jnp.concatenate([weights[first, which, :ROWS], weights[first + 1, which, :ROWS]], 0)


def product_terms(held, weights, which, c):
    total = None
    for l in range(NL):
        rows = held[:, l, which].reshape(NX * ROWS, 2 * ROWS)
        term = dot(rows, weight_block(weights, which, l, c))
        total = term if total is None else total + term
    return total


def project_own_kernel(me_ref, own, weights, totals):
    for which in range(2):
        totals[which] = product_terms(own, weights, which, me_ref[0])


def project_kernel(me_ref, other, weights, totals, filters, gate, out, half_out):
    first = 2 * (1 - me_ref[0])
    for l in range(NL):
        for i in range(2):
            half_out[l, i] = weights[4 * l + first + i, :, :ROWS]
    for which in range(2):
        total = totals[which] + product_terms(other, weights, which, 1 - me_ref[0])
        out[:, which * NX * ROWS : (which + 1) * NX * ROWS] = total.T.astype(bf16)
    base = 2 * NX * ROWS
    out[:, base : base + ROWS] = filters[...].astype(f32).T.astype(bf16)
    out[:, base + ROWS : base + 2 * ROWS] = gate[...].astype(f32).T.astype(bf16)


def convolve_kernel(
    got, first, first_back, twist_cos, twist_sin, second, second_back, out,
    proj, gmod, filt, gate, mixed, spectrum, product, back, o_mod, o_gp, o_gg,
):
    half = NX * ROWS

    def lanes(start):
        return slice(start, start + ROWS)

    for y in range(NY):
        for x in range(NX):
            b = x * NY + y
            at = slice(b * OWN, (b + 1) * OWN)
            for base, held in ((0, proj), (half, gmod)):
                total = got[y, :, lanes(base + x * ROWS)].astype(f32)
                for k in range(1, NX):
                    total = total + got[k * NY + y, :, lanes(base + x * ROWS)].astype(f32)
                held[at, :] = total
            filt[at, :] = got[b, :, lanes(2 * half)].astype(f32)
            gate[at, :] = got[b, :, lanes(2 * half + ROWS)].astype(f32)
    cosine, sine = twist_cos[...], twist_sin[...]
    for c in range(OWN):
        pick = pl.ds(c, BLOCKS, stride=OWN)
        signals = jnp.concatenate(
            [
                proj[pick, :].astype(bf16),
                (gmod[pick, :] * gate[pick, :]).astype(bf16),
                filt[pick, :].astype(bf16),
            ],
            1,
        )
        parts = dot(first[...], signals)
        for i in range(3):
            real = parts[:FREQS, lanes(i * ROWS)]
            imag = parts[FREQS:, lanes(i * ROWS)]
            at = slice((c * 3 + i) * FREQS, (c * 3 + i + 1) * FREQS)
            mixed[at, :ROWS] = (real * cosine + imag * sine).astype(bf16)
            mixed[at, ROWS:] = (imag * cosine - real * sine).astype(bf16)
    spectrum[...] = dot(mixed[...], second[...])
    for c in range(OWN):
        (xr, xi), (gr, gi), (hr, hi) = [
            (spectrum[at, :ROWS], spectrum[at, ROWS:])
            for at in [slice((c * 3 + i) * FREQS, (c * 3 + i + 1) * FREQS) for i in range(3)]
        ]
        at = slice(2 * c * FREQS, (2 * c + 1) * FREQS)
        product[at, :ROWS] = (xr * hr - xi * hi).astype(bf16)
        product[at, ROWS:] = (xr * hi + xi * hr).astype(bf16)
        at = slice((2 * c + 1) * FREQS, (2 * c + 2) * FREQS)
        product[at, :ROWS] = (gr * hr + gi * hi).astype(bf16)
        product[at, ROWS:] = (gi * hr - gr * hi).astype(bf16)
    back[...] = dot(product[...], second_back[...])
    for c in range(OWN):
        pick = pl.ds(c, BLOCKS, stride=OWN)
        columns = []
        for i in range(2):
            at = slice((2 * c + i) * FREQS, (2 * c + i + 1) * FREQS)
            real, imag = back[at, :ROWS], back[at, ROWS:]
            columns.append(
                jnp.concatenate(
                    [
                        (real * cosine - imag * sine).astype(bf16),
                        (imag * cosine + real * sine).astype(bf16),
                    ],
                    0,
                )
            )
        in_time = dot(first_back[...], jnp.concatenate(columns, 1)) * (1.0 / LENGTH)
        convolved = in_time[:, :ROWS]
        o_gp[pick, :] = in_time[:, ROWS:]
        o_mod[pick, :] = gate[pick, :] * convolved
        o_gg[pick, :] = gmod[pick, :] * convolved
    for y in range(NY):
        for x in range(NX):
            b = x * NY + y
            at = slice(b * OWN, (b + 1) * OWN)
            modulated = o_mod[at, :].astype(bf16)
            grad = o_gp[at, :].astype(bf16)
            for k in range(NX):
                out[k * NY + y, :, lanes(x * ROWS)] = modulated
                out[k * NY + y, :, lanes(half + x * ROWS)] = grad
            out[b, :, lanes(2 * half)] = o_gg[at, :].astype(bf16)


def weight_grad_kernel(me_ref, got, own, other, out):
    me = me_ref[0]
    half = NX * ROWS
    for which in range(2):
        left = got[:, half:] if which == 0 else got[:, :half]
        for l in range(NL):
            for held, c in ((own, me), (other, 1 - me)):
                rows = held[:, l, which].reshape(half, 2 * ROWS)
                total = dot(left, rows).astype(bf16)
                out[4 * l + 2 * c, which] = total[:, :ROWS]
                out[4 * l + 2 * c + 1, which] = total[:, ROWS:]


def output_kernel(me_ref, got, got_other, weights, weights_other, out):
    half = NX * ROWS
    for which in range(2):
        lanes = slice(which * half, (which + 1) * half)
        rows = [held[:, lanes].astype(f32).T.astype(bf16) for held in (got, got_other)]
        for l in range(NL):
            other = [weights_other[l, i, 1 - which] for i in range(2)]
            blocks = (weight_block(weights, 1 - which, l, me_ref[0]), jnp.concatenate(other, 0))
            total = None
            for left, right in zip(rows, blocks):
                term = lax.dot_general(
                    left, right, (((1,), (1,)), ((), ())), preferred_element_type=f32
                )
                total = term if total is None else total + term
            out[:, l, which] = total.astype(bf16).reshape(NX, ROWS, 2 * ROWS)


def call(kernel, inputs, out_shape, flops, scratch=(), first_smem=True):
    specs = [VMEM] * len(inputs)
    if first_smem:
        specs[0] = SMEM
    many = isinstance(out_shape, tuple)
    return pl.pallas_call(
        kernel,
        out_shape=out_shape,
        in_specs=specs,
        out_specs=(VMEM,) * len(out_shape) if many else VMEM,
        scratch_shapes=list(scratch),
        compiler_params=PARAMS,
        cost_estimate=pl.CostEstimate(
            flops=flops,
            bytes_accessed=sum(a.size * a.dtype.itemsize for a in inputs),
            transcendentals=0,
        ),
    )(*inputs)


def on_device(tokens, gate_values, filters, input_weight, output_weight, cotangent):
    tokens_here, features = tokens.shape
    channels = gate_values.shape[1]
    me = lax.axis_index("core").astype(jnp.int32).reshape(1)
    swap = swap_pairs()

    pair = jnp.pad(jnp.stack([input_weight, output_weight.T]), ((0, 0), (0, SPARE), (0, 0)))
    weights = lax.all_gather(pair, "y", axis=0)
    moved = lax.ppermute(jnp.stack([tokens, cotangent]), ALL, swap)
    copies = jnp.broadcast_to(moved[None], (NH * NL, 2, tokens_here, features))
    own = lax.all_to_all(copies, Z, split_axis=0, concat_axis=0, tiled=True)
    other = lax.ppermute(own, "core", [(0, 1), (1, 0)])
    held = (NH, NL, 2, tokens_here, features)
    own, other = own.reshape(held), other.reshape(held)

    half = NX * ROWS
    totals = call(
        project_own_kernel,
        (me, own, weights),
        jax.ShapeDtypeStruct((2, half, channels), f32),
        160 * half * 512 * channels,
    )
    sent, weights_half = call(
        project_kernel,
        (me, other, weights, totals, filters, gate_values),
        (
            jax.ShapeDtypeStruct((channels, 2 * half + 2 * ROWS), bf16),
            jax.ShapeDtypeStruct((NL, 2, 2, ROWS, channels), bf16),
        ),
        4 * half * 512 * channels,
    )
    weights_other = lax.ppermute(weights_half, "core", [(0, 1), (1, 0)])
    got = lax.all_to_all(
        sent.reshape(BLOCKS, OWN, 2 * half + 2 * ROWS), CTX, split_axis=0, concat_axis=0, tiled=True
    )
    per_channel = pltpu.VMEM((BLOCKS * OWN, ROWS), f32)
    sent = call(
        convolve_kernel,
        (got,) + tables(),
        jax.ShapeDtypeStruct((BLOCKS, OWN, 2 * half + ROWS), bf16),
        2 * 40 * OWN * FREQS * 256 * 256,
        [per_channel] * 4
        + [
            pltpu.VMEM((3 * OWN * FREQS, 2 * ROWS), bf16),
            pltpu.VMEM((3 * OWN * FREQS, 2 * ROWS), f32),
            pltpu.VMEM((2 * OWN * FREQS, 2 * ROWS), bf16),
            pltpu.VMEM((2 * OWN * FREQS, 2 * ROWS), f32),
        ]
        + [per_channel] * 3,
        first_smem=False,
    )
    got = lax.all_to_all(sent, CTX, split_axis=0, concat_axis=0, tiled=True)
    got = got.reshape(channels, 2 * half + ROWS)
    streams, grad_gate = got[:, : 2 * half], got[:, 2 * half :].T

    grads = call(
        weight_grad_kernel,
        (me, streams, own, other),
        jax.ShapeDtypeStruct((NY, 2, channels, ROWS), bf16),
        4 * half * 1024 * channels,
    )
    grads = lax.psum_scatter(grads, "y", scatter_dimension=0, tiled=True)
    grad_input_weight, grad_output_weight = grads[0, 0].T, grads[0, 1]

    streams_other = lax.ppermute(streams, "core", [(0, 1), (1, 0)])
    parts = call(
        output_kernel,
        (me, streams, streams_other, weights, weights_other),
        jax.ShapeDtypeStruct(held, bf16),
        4 * half * 1024 * channels,
    )
    parts = lax.all_to_all(
        parts.reshape(NH * NL, 2, tokens_here, features), Z, split_axis=0, concat_axis=0, tiled=True
    )
    total = jnp.sum(parts.astype(f32), 0).astype(bf16)
    total = lax.ppermute(total, ALL, swap)
    return (total[0], total[1], grad_gate, grad_input_weight, grad_output_weight)


def solution(mesh):
    chips = Mesh(mesh.devices.reshape(NX, NY, NH, NL, NC), ALL)
    rows, columns = P(CTX, TP), P(TP, CTX)
    return jax.shard_map(
        on_device,
        mesh=chips,
        in_specs=(rows, rows, rows, rows, columns, rows),
        out_specs=(rows, rows, rows, rows, columns),
        check_vma=False,
    )
```

```python
import math

import jax
import jax.numpy as jnp
import numpy as np
from jax import lax
from jax.experimental import pallas as pl
from jax.experimental.pallas import tpu as pltpu
from jax.sharding import Mesh, PartitionSpec as P

bf16 = jnp.bfloat16
f32 = jnp.float32

NX, NY, NH, NL, NC = 4, 8, 4, 2, 2
CTX = ("x", "y")
TP = ("zh", "zl", "core")
ALL = CTX + TP
Z = ("zh", "zl")

BLOCKS = NX * NY
ROWS = 128
FREQS = 2 * BLOCKS
LENGTH = FREQS * ROWS
SPARE = 8
OWN = 8

VMEM = pl.BlockSpec(memory_space=pltpu.VMEM)
SMEM = pl.BlockSpec(memory_space=pltpu.SMEM)
PARAMS = pltpu.CompilerParams(vmem_limit_bytes=48 * 1024 * 1024)


def swap_pairs():
    def place(x, y, h, l, c):
        return (((x * NY + y) * NH + h) * NL + l) * NC + c

    return [
        (place(x, y, h, l, c), place(h, y, x, l, c))
        for x in range(NX)
        for y in range(NY)
        for h in range(NH)
        for l in range(NL)
        for c in range(NC)
    ]


def tables():
    freq = np.arange(FREQS)
    block = np.arange(BLOCKS)
    row = np.arange(ROWS)
    angle = 2 * math.pi * (freq[:, None] * block[None, :] % FREQS) / FREQS
    first = np.concatenate([np.cos(angle), -np.sin(angle)], 0)
    twist = 2 * math.pi * (freq[:, None] * row[None, :] % LENGTH) / LENGTH
    angle = 2 * math.pi * (row[:, None] * row[None, :] % ROWS) / ROWS
    cosine, sine = np.cos(angle), np.sin(angle)
    second = np.block([[cosine, -sine], [sine, cosine]])
    return (
        jnp.asarray(first, bf16),
        jnp.asarray(first.T, bf16),
        jnp.asarray(np.cos(twist), f32),
        jnp.asarray(np.sin(twist), f32),
        jnp.asarray(second, bf16),
        jnp.asarray(second.T, bf16),
    )


def dot(left, right):
    return jnp.dot(left, right, preferred_element_type=f32)


def weight_block(weights, which, l, c):
    first = 4 * l + 2 * c
    return jnp.concatenate([weights[first, which, :ROWS], weights[first + 1, which, :ROWS]], 0)


def product_terms(held, weights, which, c):
    total = None
    for l in range(NL):
        rows = held[:, l, which].reshape(NX * ROWS, 2 * ROWS)
        term = dot(rows, weight_block(weights, which, l, c))
        total = term if total is None else total + term
    return total


def project_own_kernel(me_ref, own, weights, totals):
    for which in range(2):
        totals[which] = product_terms(own, weights, which, me_ref[0])


def project_kernel(me_ref, other, weights, totals, filters, gate, out):
    for which in range(2):
        total = totals[which] + product_terms(other, weights, which, 1 - me_ref[0])
        out[:, which * NX * ROWS : (which + 1) * NX * ROWS] = total.T.astype(bf16)
    base = 2 * NX * ROWS
    out[:, base : base + ROWS] = filters[...].astype(f32).T.astype(bf16)
    out[:, base + ROWS : base + 2 * ROWS] = gate[...].astype(f32).T.astype(bf16)


def convolve_kernel(
    got, first, first_back, twist_cos, twist_sin, second, second_back, out,
    proj, gmod, filt, gate, mixed, spectrum, product, back, o_mod, o_gp, o_gg,
):
    half = NX * ROWS

    def lanes(start):
        return slice(start, start + ROWS)

    for y in range(NY):
        for x in range(NX):
            b = x * NY + y
            at = slice(b * OWN, (b + 1) * OWN)
            for base, held in ((0, proj), (half, gmod)):
                total = got[y, :, lanes(base + x * ROWS)].astype(f32)
                for k in range(1, NX):
                    total = total + got[k * NY + y, :, lanes(base + x * ROWS)].astype(f32)
                held[at, :] = total
            filt[at, :] = got[b, :, lanes(2 * half)].astype(f32)
            gate[at, :] = got[b, :, lanes(2 * half + ROWS)].astype(f32)
    cosine, sine = twist_cos[...], twist_sin[...]
    for c in range(OWN):
        pick = pl.ds(c, BLOCKS, stride=OWN)
        signals = jnp.concatenate(
            [
                proj[pick, :].astype(bf16),
                (gmod[pick, :] * gate[pick, :]).astype(bf16),
                filt[pick, :].astype(bf16),
            ],
            1,
        )
        parts = dot(first[...], signals)
        for i in range(3):
            real = parts[:FREQS, lanes(i * ROWS)]
            imag = parts[FREQS:, lanes(i * ROWS)]
            at = slice((c * 3 + i) * FREQS, (c * 3 + i + 1) * FREQS)
            mixed[at, :ROWS] = (real * cosine + imag * sine).astype(bf16)
            mixed[at, ROWS:] = (imag * cosine - real * sine).astype(bf16)
    spectrum[...] = dot(mixed[...], second[...])
    for c in range(OWN):
        (xr, xi), (gr, gi), (hr, hi) = [
            (spectrum[at, :ROWS], spectrum[at, ROWS:])
            for at in [slice((c * 3 + i) * FREQS, (c * 3 + i + 1) * FREQS) for i in range(3)]
        ]
        at = slice(2 * c * FREQS, (2 * c + 1) * FREQS)
        product[at, :ROWS] = (xr * hr - xi * hi).astype(bf16)
        product[at, ROWS:] = (xr * hi + xi * hr).astype(bf16)
        at = slice((2 * c + 1) * FREQS, (2 * c + 2) * FREQS)
        product[at, :ROWS] = (gr * hr + gi * hi).astype(bf16)
        product[at, ROWS:] = (gi * hr - gr * hi).astype(bf16)
    back[...] = dot(product[...], second_back[...])
    for c in range(OWN):
        pick = pl.ds(c, BLOCKS, stride=OWN)
        columns = []
        for i in range(2):
            at = slice((2 * c + i) * FREQS, (2 * c + i + 1) * FREQS)
            real, imag = back[at, :ROWS], back[at, ROWS:]
            columns.append(
                jnp.concatenate(
                    [
                        (real * cosine - imag * sine).astype(bf16),
                        (imag * cosine + real * sine).astype(bf16),
                    ],
                    0,
                )
            )
        in_time = dot(first_back[...], jnp.concatenate(columns, 1)) * (1.0 / LENGTH)
        convolved = in_time[:, :ROWS]
        o_gp[pick, :] = in_time[:, ROWS:]
        o_mod[pick, :] = gate[pick, :] * convolved
        o_gg[pick, :] = gmod[pick, :] * convolved
    for y in range(NY):
        for x in range(NX):
            b = x * NY + y
            at = slice(b * OWN, (b + 1) * OWN)
            modulated = o_mod[at, :].astype(bf16)
            grad = o_gp[at, :].astype(bf16)
            for k in range(NX):
                out[k * NY + y, :, lanes(x * ROWS)] = modulated
                out[k * NY + y, :, lanes(half + x * ROWS)] = grad
            out[b, :, lanes(2 * half)] = o_gg[at, :].astype(bf16)


def weight_grad_kernel(me_ref, got, own, other, out):
    me = me_ref[0]
    half = NX * ROWS
    for which in range(2):
        left = got[:, half:] if which == 0 else got[:, :half]
        for l in range(NL):
            for held, c in ((own, me), (other, 1 - me)):
                rows = held[:, l, which].reshape(half, 2 * ROWS)
                total = dot(left, rows).astype(bf16)
                out[4 * l + 2 * c, which] = total[:, :ROWS]
                out[4 * l + 2 * c + 1, which] = total[:, ROWS:]


def output_terms(got, weights, which, l, c):
    half = NX * ROWS
    rows = got[:, which * half : (which + 1) * half].astype(f32).T.astype(bf16)
    block = weight_block(weights, 1 - which, l, c)
    total = lax.dot_general(rows, block, (((1,), (1,)), ((), ())), preferred_element_type=f32)
    return total.reshape(NX, ROWS, 2 * ROWS)


def send_kernel(me_ref, got, weights, send):
    for which in range(2):
        for l in range(NL):
            send[:, l, which] = output_terms(got, weights, which, l, 1 - me_ref[0]).astype(bf16)


def keep_kernel(me_ref, got, weights, arrived, out):
    for which in range(2):
        for l in range(NL):
            total = output_terms(got, weights, which, l, me_ref[0])
            out[:, l, which] = (total + arrived[:, l, which].astype(f32)).astype(bf16)


def call(kernel, inputs, out_shape, flops, scratch=(), first_smem=True):
    specs = [VMEM] * len(inputs)
    if first_smem:
        specs[0] = SMEM
    many = isinstance(out_shape, tuple)
    return pl.pallas_call(
        kernel,
        out_shape=out_shape,
        in_specs=specs,
        out_specs=(VMEM,) * len(out_shape) if many else VMEM,
        scratch_shapes=list(scratch),
        compiler_params=PARAMS,
        cost_estimate=pl.CostEstimate(
            flops=flops,
            bytes_accessed=sum(a.size * a.dtype.itemsize for a in inputs),
            transcendentals=0,
        ),
    )(*inputs)


def on_device(tokens, gate_values, filters, input_weight, output_weight, cotangent):
    tokens_here, features = tokens.shape
    channels = gate_values.shape[1]
    me = lax.axis_index("core").astype(jnp.int32).reshape(1)
    swap = swap_pairs()

    pair = jnp.pad(jnp.stack([input_weight, output_weight.T]), ((0, 0), (0, SPARE), (0, 0)))
    weights = lax.all_gather(pair, "y", axis=0)
    moved = lax.ppermute(jnp.stack([tokens, cotangent]), ALL, swap)
    copies = jnp.broadcast_to(moved[None], (NH * NL, 2, tokens_here, features))
    own = lax.all_to_all(copies, Z, split_axis=0, concat_axis=0, tiled=True)
    other = lax.ppermute(own, "core", [(0, 1), (1, 0)])
    held = (NH, NL, 2, tokens_here, features)
    own, other = own.reshape(held), other.reshape(held)

    half = NX * ROWS
    totals = call(
        project_own_kernel,
        (me, own, weights),
        jax.ShapeDtypeStruct((2, half, channels), f32),
        160 * half * 512 * channels,
    )
    sent = call(
        project_kernel,
        (me, other, weights, totals, filters, gate_values),
        jax.ShapeDtypeStruct((channels, 2 * half + 2 * ROWS), bf16),
        4 * half * 512 * channels,
    )
    got = lax.all_to_all(
        sent.reshape(BLOCKS, OWN, 2 * half + 2 * ROWS), CTX, split_axis=0, concat_axis=0, tiled=True
    )
    per_channel = pltpu.VMEM((BLOCKS * OWN, ROWS), f32)
    sent = call(
        convolve_kernel,
        (got,) + tables(),
        jax.ShapeDtypeStruct((BLOCKS, OWN, 2 * half + ROWS), bf16),
        2 * 40 * OWN * FREQS * 256 * 256,
        [per_channel] * 4
        + [
            pltpu.VMEM((3 * OWN * FREQS, 2 * ROWS), bf16),
            pltpu.VMEM((3 * OWN * FREQS, 2 * ROWS), f32),
            pltpu.VMEM((2 * OWN * FREQS, 2 * ROWS), bf16),
            pltpu.VMEM((2 * OWN * FREQS, 2 * ROWS), f32),
        ]
        + [per_channel] * 3,
        first_smem=False,
    )
    got = lax.all_to_all(sent, CTX, split_axis=0, concat_axis=0, tiled=True)
    got = got.reshape(channels, 2 * half + ROWS)
    streams, grad_gate = got[:, : 2 * half], got[:, 2 * half :].T

    grads = call(
        weight_grad_kernel,
        (me, streams, own, other),
        jax.ShapeDtypeStruct((NY, 2, channels, ROWS), bf16),
        4 * half * 1024 * channels,
    )
    grads = lax.psum_scatter(grads, "y", scatter_dimension=0, tiled=True)
    grad_input_weight, grad_output_weight = grads[0, 0].T, grads[0, 1]

    shape = jax.ShapeDtypeStruct(held, bf16)
    flops = 2 * half * 1024 * channels
    send = call(send_kernel, (me, streams, weights), shape, flops)
    arrived = lax.ppermute(send, "core", [(0, 1), (1, 0)])
    parts = call(keep_kernel, (me, streams, weights, arrived), shape, flops)
    parts = lax.all_to_all(
        parts.reshape(NH * NL, 2, tokens_here, features), Z, split_axis=0, concat_axis=0, tiled=True
    )
    total = jnp.sum(parts.astype(f32), 0).astype(bf16)
    total = lax.ppermute(total, ALL, swap)
    return (total[0], total[1], grad_gate, grad_input_weight, grad_output_weight)


def solution(mesh):
    chips = Mesh(mesh.devices.reshape(NX, NY, NH, NL, NC), ALL)
    rows, columns = P(CTX, TP), P(TP, CTX)
    return jax.shard_map(
        on_device,
        mesh=chips,
        in_specs=(rows, rows, rows, rows, columns, rows),
        out_specs=(rows, rows, rows, rows, columns),
        check_vma=False,
    )
```
